512 devices in a mesh: brow: 16 (over y, x), bcol: 32 (over z, core).
Axes of the slice: x: 4, y: 4, z: 16, core: 2. Of those that a mesh axis runs over, the one named last changes fastest.
Arguments:
- gradient: bfloat16 [8192, 8192], P(('brow', 'bcol')), may hold values from -1.5 to 1.5
- left_stats: float32 [16, 8192, 512], P('brow', 'bcol'), may hold values from -1 to 8, as said below
- right_stats: float32 [16, 8192, 512], P('brow', 'bcol'), may hold values from -1 to 8, as said below
- left_roots: bfloat16 [16, 8192, 512], P('brow', 'bcol'), may hold values from -1 to 3, as said below
- right_roots: bfloat16 [16, 8192, 512], P('brow', 'bcol'), may hold values from -1 to 3, as said below
- refresh: int32 [16, 4], P('brow'), may hold values from 0 to 15, as said below
Outputs:
- update: bfloat16 [8192, 8192], P(('brow', 'bcol'))
- new_left_stats: float32 [16, 8192, 512], P('brow', 'bcol')
- new_right_stats: float32 [16, 8192, 512], P('brow', 'bcol')
- new_left_roots: bfloat16 [16, 8192, 512], P('brow', 'bcol')
- new_right_roots: bfloat16 [16, 8192, 512], P('brow', 'bcol')
The draws below stay inside these ranges and needn't reach their ends.
Inputs may be any that keep to these rules, and one draw needn't show every extreme that they name: `refresh`: each row names 4 different block columns; some block row lists column 15 and another block row lists column 0. `left_stats`: every 512 x 512 block is symmetric positive definite. `right_stats`: every 512 x 512 block is symmetric positive definite. `left_roots`: every 512 x 512 block is symmetric. `right_roots`: every 512 x 512 block is symmetric.
All inputs are finite; a program needn't handle non-finite values.
Results may differ from the reference program's by a relative error of at most 0.005.
Values may be sent and summed in bfloat16 or wider, within the bound.
A program may use at most 64 MiB of HBM per device.

```python
import math
import jax
import jax.numpy as jnp
from jax import lax

B = 512
ITERS = 3
ROW_BLOCKS = 16
COL_BLOCKS = 16
LISTED = 4
ROWS = 8192
COLS = 8192


def symmetric_blocks(key, lowest, highest_value, spread):
    first_key, second_key = jax.random.split(key)
    noise = jax.random.normal(first_key, (ROW_BLOCKS, COL_BLOCKS, B, B), jnp.float32)
    noise = (noise + jnp.swapaxes(noise, 2, 3)) * (spread / math.sqrt(2.0 * B))
    diagonal = jnp.exp(jax.random.uniform(second_key, (ROW_BLOCKS, COL_BLOCKS, B), jnp.float32, math.log(lowest), math.log(highest_value)))
    identity = jnp.eye(B, dtype=jnp.float32)
    matrix = noise + diagonal[..., None] * identity
    return matrix.reshape(ROW_BLOCKS, COL_BLOCKS * B, B)


def draw_left_stats(key, part):
    return symmetric_blocks(jax.random.fold_in(key, 11), 1.0, 3.0, 0.4)


def draw_right_stats(key, part):
    return symmetric_blocks(jax.random.fold_in(key, 23), 1.0, 3.0, 0.4)


def draw_left_roots(key, part):
    return symmetric_blocks(jax.random.fold_in(key, 37), 0.5, 1.5, 0.25).astype(jnp.bfloat16)


def draw_right_roots(key, part):
    return symmetric_blocks(jax.random.fold_in(key, 41), 0.5, 1.5, 0.25).astype(jnp.bfloat16)


def bring_front(order, target):
    moved = jnp.where(order == target, order[0], order)
    return moved.at[0].set(target)


def draw_refresh(key, part):
    row_keys = jax.random.split(jax.random.fold_in(key, 53), ROW_BLOCKS)
    orders = jax.vmap(lambda row_key: jax.random.permutation(row_key, COL_BLOCKS))(row_keys)
    orders = orders.astype(jnp.int32)
    first_key, second_key = jax.random.split(jax.random.fold_in(key, 61))
    first_row = jax.random.randint(first_key, (), 0, ROW_BLOCKS, dtype=jnp.int32)
    offset = jax.random.randint(second_key, (), 1, ROW_BLOCKS, dtype=jnp.int32)
    second_row = (first_row + offset) % ROW_BLOCKS
    last_target = jnp.full((ROW_BLOCKS,), COL_BLOCKS - 1, dtype=jnp.int32)
    zero_target = jnp.zeros((ROW_BLOCKS,), dtype=jnp.int32)
    front_last = jax.vmap(bring_front)(orders, last_target)
    front_zero = jax.vmap(bring_front)(orders, zero_target)
    row_ids = jnp.arange(ROW_BLOCKS, dtype=jnp.int32)[:, None]
    orders = jnp.where(row_ids == first_row, front_last, orders)
    orders = jnp.where(row_ids == second_row, front_zero, orders)
    return orders[:, :LISTED].astype(jnp.int32)


def block_scale(own_key, dims, shards, smallest, high):
    gain, own = 1.0, jax.random.fold_in(own_key, 6)
    for position, parts in shards:
        heights = jnp.exp(jax.random.uniform(jax.random.fold_in(own, position), (parts,), jnp.float32, smallest / len(shards), high / len(shards)))
        gain = gain * jnp.repeat(heights, dims[position] // parts).reshape([-1 if axis == position else 1 for axis in range(len(dims))])
    return gain


def scatter_about(own_key, dims, deviation, most, cuts=(), held_as=jnp.bfloat16):
    factor_of = block_scale(own_key, dims, cuts, -0.22, 0.18) if cuts else 1.0
    values = jax.random.normal(own_key, dims, jnp.float32) * deviation * factor_of
    return jnp.minimum(jnp.maximum(values, -most), most).astype(held_as)


def setup_inputs(seed: int = 0) -> dict:
    keys = jax.random.split(jax.random.key(seed), 7)
    return {
        "gradient": scatter_about(keys[0], (ROWS, COLS), 0.25, 1.5, ((0, 512),)),
        "left_stats": draw_left_stats(jax.random.fold_in(keys[6], 71), 0),
        "right_stats": draw_right_stats(jax.random.fold_in(keys[6], 71), 0),
        "left_roots": draw_left_roots(jax.random.fold_in(keys[6], 71), 0),
        "right_roots": draw_right_roots(jax.random.fold_in(keys[6], 71), 0),
        "refresh": draw_refresh(jax.random.fold_in(keys[6], 71), 0),
    }


decay = 0.9
epsilon = 1e-06
highest = lax.Precision.HIGHEST

def inverse_root(matrix):
    order_size = matrix.shape[0]
    identity = jnp.eye(order_size, dtype=jnp.float32)
    shifted = matrix + epsilon * identity
    scaling = 2.5 / jnp.sqrt(jnp.sum(shifted * shifted))
    moment = scaling * shifted
    iterate = jnp.sqrt(jnp.sqrt(scaling)) * identity
    for iteration in range(ITERS):
        factor = (5.0 * identity - moment) * 0.25
        square = jnp.dot(factor, factor, precision=highest)
        fourth = jnp.dot(square, square, precision=highest)
        moment = jnp.dot(fourth, moment, precision=highest)
        iterate = jnp.dot(iterate, factor, precision=highest)
    return iterate.astype(jnp.bfloat16)

def refresh_row(row_items):
    left_row, right_row, chosen, left_old_root, right_old_root = row_items
    picked = jnp.concatenate([left_row[chosen], right_row[chosen]], 0)
    new_roots = lax.map(inverse_root, picked).astype(jnp.float32)
    one_hot = (chosen[:, None] == jnp.arange(COL_BLOCKS, dtype=jnp.int32)[None, :]).astype(jnp.float32)
    listed = lax.optimization_barrier(jnp.sum(one_hot, 0)) > 0
    left_fresh = jnp.einsum('sc,sij->cij', one_hot, new_roots[:LISTED], precision=highest)
    right_fresh = jnp.einsum('sc,sij->cij', one_hot, new_roots[LISTED:], precision=highest)
    left_out = jnp.where(listed[:, None, None], left_fresh, left_old_root.astype(jnp.float32))
    right_out = jnp.where(listed[:, None, None], right_fresh, right_old_root.astype(jnp.float32))
    return (left_out.astype(jnp.bfloat16), right_out.astype(jnp.bfloat16))

def reference(gradient, left_stats, right_stats, left_roots, right_roots, refresh):
    blocks = gradient.reshape(ROW_BLOCKS, B, COL_BLOCKS, B).transpose(0, 2, 1, 3).astype(jnp.float32)
    left_old = left_stats.reshape(ROW_BLOCKS, COL_BLOCKS, B, B)
    right_old = right_stats.reshape(ROW_BLOCKS, COL_BLOCKS, B, B)
    left_gram = jnp.einsum('rcik,rcjk->rcij', blocks, blocks, precision=highest)
    right_gram = jnp.einsum('rcki,rckj->rcij', blocks, blocks, precision=highest)
    left_new = decay * left_old + (1.0 - decay) * left_gram
    right_new = decay * right_old + (1.0 - decay) * right_gram
    left_root_blocks = left_roots.reshape(ROW_BLOCKS, COL_BLOCKS, B, B)
    right_root_blocks = right_roots.reshape(ROW_BLOCKS, COL_BLOCKS, B, B)
    mixed = jnp.einsum('rcik,rckj->rcij', blocks, right_root_blocks.astype(jnp.float32), precision=highest)
    mixed = lax.optimization_barrier(mixed.astype(jnp.bfloat16)).astype(jnp.float32)
    update = jnp.einsum('rcik,rckj->rcij', left_root_blocks.astype(jnp.float32), mixed, precision=highest)
    update = update.astype(jnp.bfloat16).transpose(0, 2, 1, 3).reshape(ROWS, COLS)
    left_out, right_out = lax.map(refresh_row, (left_new, right_new, refresh, left_root_blocks, right_root_blocks))
    shape_out = (ROW_BLOCKS, COL_BLOCKS * B, B)
    return (update, left_new.reshape(shape_out), right_new.reshape(shape_out), left_out.reshape(shape_out), right_out.reshape(shape_out))
```

```python
import functools

import jax
import jax.numpy as jnp
from jax import lax
from jax.experimental import pallas as pl
from jax.experimental.pallas import tpu as pltpu
from jax.sharding import PartitionSpec as P

MESH = pl.DeviceIdType.MESH
bf16 = jnp.bfloat16
f32 = jnp.float32

decay = 0.9
epsilon = 1e-06
LEAD = 1.25

ROWS_BY_ROWS = (((1,), (1,)), ((), ()))
COLS_BY_COLS = (((0,), (0,)), ((), ()))


def product(left_side, right_side):
    return jnp.dot(left_side, right_side, preferred_element_type=f32)


def root_into(root_ref, stat_ref, held):
    moment, lead, tail, m16, n16, h16, p16, v16, q16 = held
    size = stat_ref.shape[0]
    a = LEAD
    diagonal = lax.broadcasted_iota(jnp.int32, (size, size), 0) == lax.broadcasted_iota(
        jnp.int32, (size, size), 1
    )
    shifted = stat_ref[...] + jnp.where(diagonal, epsilon, 0.0)
    total = jnp.sum(jnp.sum(shifted * shifted, axis=0, keepdims=True), axis=1, keepdims=True)
    scaling = 2.5 / jnp.sqrt(total)
    scale = jnp.sqrt(jnp.sqrt(scaling))
    moment[...] = shifted * scaling
    m16[...] = moment[...].astype(bf16)
    tail[...] = product(m16[...], m16[...])
    lead[...] = a * moment[...] - 0.25 * tail[...]
    h16[...] = lead[...].astype(bf16)
    tail[...] = 0.0625 * tail[...] - (0.5 * a) * moment[...]
    n16[...] = tail[...].astype(bf16)
    p16[...] = (2.0 * a * a * tail[...] + product(n16[...], n16[...])).astype(bf16)
    tail[...] = -0.25 * (a * moment[...] + a**4 * lead[...] + product(p16[...], h16[...]))
    v16[...] = tail[...].astype(bf16)
    q16[...] = (2.0 * a * a * tail[...] + product(v16[...], v16[...])).astype(bf16)
    lead[...] = a * a * moment[...] + product(v16[...], m16[...])
    h16[...] = lead[...].astype(bf16)
    lead[...] = a**4 * lead[...] + product(q16[...], h16[...])
    h16[...] = lead[...].astype(bf16)
    lead[...] = a**4 * lead[...] + product(q16[...], h16[...])
    root = jnp.where(diagonal, a**3, 0.0) + a * tail[...] - 0.25 * lead[...]
    root_ref[...] = (scale * root).astype(bf16)


def step_kernel(
    grad, left_stats, right_stats, left_roots, right_roots,
    update, new_left, new_right, fresh_left, fresh_right,
    block, left_some, right_whole, stat, other, mixed, cols, root, taken,
    moment, lead, tail, m16, n16, h16, p16, v16, q16,
    in_send, in_recv, pass_send, pass_recv, out_send, out_recv,
    pair_send, pair_recv, local_sem,
):
    slabs, slab_rows, size = block.shape
    chips, half_rows = slabs // 2, size // 2
    per_half = chips // 2
    me = lax.axis_index("bcol")
    chip, half = lax.div(me, 2), lax.rem(me, 2)
    partner = 2 * chip + (1 - half)
    near = [d * s for d in range(1, chips // 2) for s in (1, -1)] + [chips // 2]

    def peer(offset):
        return lax.rem(chip + (offset + chips), chips)

    def remote(src, dst, send, recv, target):
        return pltpu.make_async_remote_copy(
            src_ref=src, dst_ref=dst, send_sem=send, recv_sem=recv,
            device_id={"bcol": target}, device_id_type=MESH,
        )

    def columns(index):
        return pl.ds(pl.multiple_of(index * size, size), size)

    def rows_of(index):
        return pl.ds(pl.multiple_of(index * half_rows, half_rows), half_rows)

    barrier = pltpu.get_barrier_semaphore()
    for offset in near:
        pl.semaphore_signal(
            barrier, inc=1, device_id={"bcol": 2 * peer(offset) + half}, device_id_type=MESH
        )
    pl.semaphore_signal(barrier, inc=1, device_id={"bcol": partner}, device_id_type=MESH)

    own_block = pltpu.make_async_copy(grad.at[:, columns(chip)], block.at[me], local_sem.at[0])
    own_left = pltpu.make_async_copy(
        left_roots.at[:, half], left_some.at[pl.ds(half * per_half, per_half)], local_sem.at[1]
    )
    own_right = pltpu.make_async_copy(right_roots, right_whole.at[rows_of(half)], local_sem.at[2])
    own_block.start()
    own_left.start()
    own_right.start()

    @pl.when(half == 0)
    def _():
        pltpu.make_async_copy(left_stats, stat.at[rows_of(half)], local_sem.at[3]).start()
        pltpu.make_async_copy(right_stats, other, local_sem.at[4]).start()

    @pl.when(half == 1)
    def _():
        pltpu.make_async_copy(right_stats, stat.at[rows_of(half)], local_sem.at[3]).start()
        pltpu.make_async_copy(left_stats, other, local_sem.at[4]).start()

    pl.semaphore_wait(barrier, chips)

    def in_copy(to, sender):
        return remote(
            grad.at[:, columns(to)], block.at[2 * sender + half],
            in_send.at[to], in_recv.at[sender], 2 * to + half,
        )

    for offset in near[::-1]:
        in_copy(peer(offset), chip).start()

    pair_own = remote(
        grad.at[:, columns(chip)], block.at[me], pass_send.at[chip], pass_recv.at[chip], partner
    )
    pair_right = remote(
        right_roots, right_whole.at[rows_of(half)], pair_send.at[0], pair_recv.at[0], partner
    )
    pair_left = remote(
        left_roots.at[:, 1 - half], left_some.at[pl.ds(half * per_half, per_half)],
        pair_send.at[1], pair_recv.at[1], partner,
    )

    def pair_stat(source):
        return remote(source, stat.at[rows_of(half)], pair_send.at[2], pair_recv.at[2], partner)

    pair_own.start()
    pair_right.start()
    pair_left.start()

    @pl.when(half == 0)
    def _():
        pair_stat(right_stats).start()

    @pl.when(half == 1)
    def _():
        pair_stat(left_stats).start()

    def pass_on(sender):
        slot = block.at[2 * sender + half]
        return remote(slot, slot, pass_send.at[sender], pass_recv.at[sender], partner)

    def passed(sender):
        slot = block.at[2 * sender + (1 - half)]
        return remote(slot, slot, pass_send.at[sender], pass_recv.at[sender], partner)

    for offset in near:
        sender = peer(offset)
        in_copy(sender, sender).wait_recv()
        pass_on(sender).start()

    own_right.wait()
    own_left.wait()
    own_block.wait()
    remote(
        right_roots, right_whole.at[rows_of(1 - half)], pair_send.at[0], pair_recv.at[0], partner
    ).wait_recv()
    remote(
        left_roots.at[:, 1 - half], left_some.at[pl.ds((1 - half) * per_half, per_half)],
        pair_send.at[1], pair_recv.at[1], partner,
    ).wait_recv()
    passed(chip).wait_recv()
    for offset in near:
        passed(peer(offset)).wait_recv()

    whole = block[...].reshape(size, size)
    mixed[...] = product(whole, right_whole[...]).astype(bf16)
    cols[...] = (
        product(left_some[...].reshape(half_rows, size), mixed[...])
        .astype(bf16)
        .reshape(cols.shape)
    )

    def out_copy(to, sender):
        return remote(
            cols.at[to], update.at[:, columns(sender)], out_send.at[to], out_recv.at[sender],
            2 * to + half,
        )

    for offset in near[::-1]:
        out_copy(peer(offset), chip).start()
    keep = pltpu.make_async_copy(cols.at[chip], update.at[:, columns(chip)], local_sem.at[5])
    keep.start()

    remote(
        left_stats, stat.at[rows_of(1 - half)], pair_send.at[2], pair_recv.at[2], partner
    ).wait_recv()
    pltpu.make_async_copy(left_stats, stat.at[rows_of(half)], local_sem.at[3]).wait()
    pltpu.make_async_copy(right_stats, other, local_sem.at[4]).wait()

    def blend(old, gram):
        return decay * old + (1.0 - decay) * gram

    @pl.when(half == 0)
    def _():
        g = block[...].reshape(size, size)
        stat[...] = blend(
            stat[...], lax.dot_general(g, g, ROWS_BY_ROWS, preferred_element_type=f32)
        )
        new_left[...] = stat[:half_rows]
        new_right[...] = blend(
            other[...],
            lax.dot_general(g[:, :half_rows], g, COLS_BY_COLS, preferred_element_type=f32),
        )

    @pl.when(half == 1)
    def _():
        g = block[...].reshape(size, size)
        stat[...] = blend(
            stat[...], lax.dot_general(g, g, COLS_BY_COLS, preferred_element_type=f32)
        )
        new_right[...] = stat[half_rows:]
        new_left[...] = blend(
            other[...],
            lax.dot_general(g[half_rows:], g, ROWS_BY_ROWS, preferred_element_type=f32),
        )

    root_into(root, stat, (moment, lead, tail, m16, n16, h16, p16, v16, q16))
    give = remote(root.at[rows_of(1 - half)], taken, pair_send.at[3], pair_recv.at[3], partner)
    give.start()

    @pl.when(half == 0)
    def _():
        fresh_left[...] = root[:half_rows]

    @pl.when(half == 1)
    def _():
        fresh_right[...] = root[half_rows:]

    give.wait_recv()

    @pl.when(half == 0)
    def _():
        fresh_right[...] = taken[...]

    @pl.when(half == 1)
    def _():
        fresh_left[...] = taken[...]

    keep.wait()
    for offset in near:
        out_copy(peer(offset), peer(offset)).wait_recv()
    for offset in near:
        in_copy(peer(offset), chip).wait_send()
        pass_on(peer(offset)).wait_send()
        out_copy(peer(offset), chip).wait_send()
    pair_own.wait_send()
    pair_right.wait_send()
    pair_left.wait_send()
    pair_stat(left_stats).wait_send()
    give.wait_send()


def final_kernel(
    refresh, update, new_left, new_right, fresh_left, fresh_right, old_left, old_right,
    update_out, left_out, right_out, left_root, right_root, chosen, sems,
):
    block_col = lax.div(lax.axis_index("bcol"), 2)
    fetched = pltpu.make_async_copy(refresh, chosen, sems.at[5])
    fetched.start()
    sure = [
        pltpu.make_async_copy(update, update_out, sems.at[0]),
        pltpu.make_async_copy(new_left, left_out, sems.at[1]),
        pltpu.make_async_copy(new_right, right_out, sems.at[2]),
    ]
    for copy in sure:
        copy.start()
    fetched.wait()
    listed = chosen[0, 0] == block_col
    for place in range(1, chosen.shape[1]):
        listed = jnp.logical_or(listed, chosen[0, place] == block_col)

    @pl.when(listed)
    def _():
        pltpu.make_async_copy(fresh_left, left_root, sems.at[3]).start()
        pltpu.make_async_copy(fresh_right, right_root, sems.at[4]).start()

    @pl.when(jnp.logical_not(listed))
    def _():
        pltpu.make_async_copy(old_left, left_root, sems.at[3]).start()
        pltpu.make_async_copy(old_right, right_root, sems.at[4]).start()

    for copy in sure:
        copy.wait()
    pltpu.make_async_copy(fresh_left, left_root, sems.at[3]).wait()
    pltpu.make_async_copy(fresh_right, right_root, sems.at[4]).wait()


def body(chips, gradient, left_stats, right_stats, left_roots, right_roots, refresh):
    slab_rows, half_rows, size = gradient.shape[0], left_stats.shape[1], left_stats.shape[2]
    width = gradient.shape[1]
    per_half = chips // 2
    place = functools.partial(pltpu.with_memory_space_constraint, memory_space=pltpu.HBM)
    in_hbm = pl.BlockSpec(memory_space=pltpu.HBM)
    in_vmem = pl.BlockSpec(memory_space=pltpu.VMEM)
    shaped = jax.ShapeDtypeStruct
    dma = pltpu.SemaphoreType.DMA
    square32, square16 = pltpu.VMEM((size, size), f32), pltpu.VMEM((size, size), bf16)
    stat_half = shaped((half_rows, size), f32)
    root_half = shaped((half_rows, size), bf16)
    results = pl.pallas_call(
        step_kernel,
        out_shape=(shaped((slab_rows, width), bf16), stat_half, stat_half, root_half, root_half),
        in_specs=[in_hbm] * 5,
        out_specs=[in_vmem] * 5,
        scratch_shapes=[
            pltpu.VMEM((2 * chips, slab_rows, size), bf16),
            pltpu.VMEM((chips, slab_rows, size), bf16),
            square16,
            square32,
            pltpu.VMEM((half_rows, size), f32),
            square16,
            pltpu.VMEM((chips, slab_rows, size), bf16),
            square16,
            pltpu.VMEM((half_rows, size), bf16),
            square32, square32, square32,
            square16, square16, square16, square16, square16, square16,
            dma((chips,)), dma((chips,)), dma((chips,)), dma((chips,)),
            dma((chips,)), dma((chips,)), dma((4,)), dma((4,)), dma((6,)),
        ],
        compiler_params=pltpu.CompilerParams(
            collective_id=0, has_side_effects=True, vmem_limit_bytes=40 * 2**20
        ),
        name="exchange",
    )(
        place(gradient),
        place(left_stats[0]),
        place(right_stats[0]),
        place(left_roots.reshape(per_half, 2, slab_rows, size)),
        place(right_roots[0]),
    )
    outputs = pl.pallas_call(
        final_kernel,
        out_shape=(shaped((slab_rows, width), bf16), stat_half, stat_half, root_half, root_half),
        in_specs=[in_hbm] + [pl.BlockSpec(memory_space=pl.ANY)] * 5 + [in_hbm] * 2,
        out_specs=[in_hbm] * 5,
        scratch_shapes=[pltpu.SMEM(refresh.shape, jnp.int32), dma((6,))],
        compiler_params=pltpu.CompilerParams(vmem_limit_bytes=2**20),
        name="place",
    )(place(refresh), *results, place(left_roots[0]), place(right_roots[0]))
    return (outputs[0],) + tuple(out[None] for out in outputs[1:])


def solution(mesh):
    rows, blocks = P(("brow", "bcol"), None), P("brow", "bcol", None)
    return jax.shard_map(
        functools.partial(body, mesh.shape["bcol"] // 2),
        mesh=mesh,
        in_specs=(rows, blocks, blocks, blocks, blocks, P("brow", None)),
        out_specs=(rows, blocks, blocks, blocks, blocks),
        check_vma=False,
    )
```

```python
import functools

import jax
import jax.numpy as jnp
from jax import lax
from jax.experimental import pallas as pl
from jax.experimental.pallas import tpu as pltpu
from jax.sharding import PartitionSpec as P

MESH = pl.DeviceIdType.MESH
bf16 = jnp.bfloat16
f32 = jnp.float32

decay = 0.9
epsilon = 1e-06
LEAD = 1.25

ROWS_BY_ROWS = (((1,), (1,)), ((), ()))
COLS_BY_COLS = (((0,), (0,)), ((), ()))


def product(left_side, right_side):
    return jnp.dot(left_side, right_side, preferred_element_type=f32)


def root_into(root_ref, stat_ref, held):
    moment, lead, tail, m16, n16, h16, p16, v16, q16 = held
    size = stat_ref.shape[0]
    a = LEAD
    diagonal = lax.broadcasted_iota(jnp.int32, (size, size), 0) == lax.broadcasted_iota(
        jnp.int32, (size, size), 1
    )
    shifted = stat_ref[...] + jnp.where(diagonal, epsilon, 0.0)
    total = jnp.sum(jnp.sum(shifted * shifted, axis=0, keepdims=True), axis=1, keepdims=True)
    scaling = 2.5 / jnp.sqrt(total)
    scale = jnp.sqrt(jnp.sqrt(scaling))
    moment[...] = shifted * scaling
    m16[...] = moment[...].astype(bf16)
    tail[...] = product(m16[...], m16[...])
    lead[...] = a * moment[...] - 0.25 * tail[...]
    h16[...] = lead[...].astype(bf16)
    tail[...] = 0.0625 * tail[...] - (0.5 * a) * moment[...]
    n16[...] = tail[...].astype(bf16)
    p16[...] = (2.0 * a * a * tail[...] + product(n16[...], n16[...])).astype(bf16)
    tail[...] = -0.25 * (a * moment[...] + a**4 * lead[...] + product(p16[...], h16[...]))
    v16[...] = tail[...].astype(bf16)
    q16[...] = (2.0 * a * a * tail[...] + product(v16[...], v16[...])).astype(bf16)
    lead[...] = a * a * moment[...] + product(v16[...], m16[...])
    h16[...] = lead[...].astype(bf16)
    lead[...] = a**4 * lead[...] + product(q16[...], h16[...])
    h16[...] = lead[...].astype(bf16)
    lead[...] = a**4 * lead[...] + product(q16[...], h16[...])
    root = jnp.where(diagonal, a**3, 0.0) + a * tail[...] - 0.25 * lead[...]
    root_ref[...] = (scale * root).astype(bf16)


def step_kernel(
    grad, left_stats, right_stats, left_roots, right_roots,
    update, new_left, new_right, fresh_left, fresh_right,
    block, left_some, right_whole, stat, other, mixed, cols, root, taken,
    moment, lead, tail, m16, n16, h16, p16, v16, q16,
    in_send, in_recv, pass_send, pass_recv, out_send, out_recv,
    pair_send, pair_recv, local_sem,
):
    slabs, slab_rows, size = block.shape
    chips, half_rows = slabs // 2, size // 2
    per_half = chips // 2
    me = lax.axis_index("bcol")
    chip, half = lax.div(me, 2), lax.rem(me, 2)
    partner = 2 * chip + (1 - half)
    near = [d * s for d in range(1, chips // 2) for s in (1, -1)] + [chips // 2]

    def peer(offset):
        return lax.rem(chip + (offset + chips), chips)

    def remote(src, dst, send, recv, target):
        return pltpu.make_async_remote_copy(
            src_ref=src, dst_ref=dst, send_sem=send, recv_sem=recv,
            device_id={"bcol": target}, device_id_type=MESH,
        )

    def in_turn(send, first):
        for parity in (0, 1):

            @pl.when(lax.rem(chip, 2) == parity)
            def _():
                for turn in (first, 1 - first):
                    for offset in near[::-1]:
                        if (parity + offset) % 2 == turn:
                            send(peer(offset))

    def columns(index):
        return pl.ds(pl.multiple_of(index * size, size), size)

    def rows_of(index):
        return pl.ds(pl.multiple_of(index * half_rows, half_rows), half_rows)

    barrier = pltpu.get_barrier_semaphore()
    for offset in near:
        pl.semaphore_signal(
            barrier, inc=1, device_id={"bcol": 2 * peer(offset) + half}, device_id_type=MESH
        )
    pl.semaphore_signal(barrier, inc=1, device_id={"bcol": partner}, device_id_type=MESH)

    own_block = pltpu.make_async_copy(grad.at[:, columns(chip)], block.at[me], local_sem.at[0])
    own_left = pltpu.make_async_copy(
        left_roots.at[:, half], left_some.at[pl.ds(half * per_half, per_half)], local_sem.at[1]
    )
    own_right = pltpu.make_async_copy(right_roots, right_whole.at[rows_of(half)], local_sem.at[2])
    own_block.start()
    own_left.start()
    own_right.start()

    @pl.when(half == 0)
    def _():
        pltpu.make_async_copy(left_stats, stat.at[rows_of(half)], local_sem.at[3]).start()
        pltpu.make_async_copy(right_stats, other, local_sem.at[4]).start()

    @pl.when(half == 1)
    def _():
        pltpu.make_async_copy(right_stats, stat.at[rows_of(half)], local_sem.at[3]).start()
        pltpu.make_async_copy(left_stats, other, local_sem.at[4]).start()

    pl.semaphore_wait(barrier, chips)

    def in_copy(to, sender):
        return remote(
            grad.at[:, columns(to)], block.at[2 * sender + half],
            in_send.at[to], in_recv.at[sender], 2 * to + half,
        )

    in_turn(lambda to: in_copy(to, chip).start(), 0)

    pair_own = remote(
        grad.at[:, columns(chip)], block.at[me], pass_send.at[chip], pass_recv.at[chip], partner
    )
    pair_right = remote(
        right_roots, right_whole.at[rows_of(half)], pair_send.at[0], pair_recv.at[0], partner
    )
    pair_left = remote(
        left_roots.at[:, 1 - half], left_some.at[pl.ds(half * per_half, per_half)],
        pair_send.at[1], pair_recv.at[1], partner,
    )

    def pair_stat(source):
        return remote(source, stat.at[rows_of(half)], pair_send.at[2], pair_recv.at[2], partner)

    pair_own.start()
    pair_right.start()
    pair_left.start()

    @pl.when(half == 0)
    def _():
        pair_stat(right_stats).start()

    @pl.when(half == 1)
    def _():
        pair_stat(left_stats).start()

    def pass_on(sender):
        slot = block.at[2 * sender + half]
        return remote(slot, slot, pass_send.at[sender], pass_recv.at[sender], partner)

    def passed(sender):
        slot = block.at[2 * sender + (1 - half)]
        return remote(slot, slot, pass_send.at[sender], pass_recv.at[sender], partner)

    for offset in near[::-1]:
        sender = peer(offset)
        in_copy(sender, sender).wait_recv()
        pass_on(sender).start()

    own_right.wait()
    own_left.wait()
    own_block.wait()
    remote(
        right_roots, right_whole.at[rows_of(1 - half)], pair_send.at[0], pair_recv.at[0], partner
    ).wait_recv()
    remote(
        left_roots.at[:, 1 - half], left_some.at[pl.ds((1 - half) * per_half, per_half)],
        pair_send.at[1], pair_recv.at[1], partner,
    ).wait_recv()
    passed(chip).wait_recv()
    for offset in near:
        passed(peer(offset)).wait_recv()

    whole = block[...].reshape(size, size)
    mixed[...] = product(whole, right_whole[...]).astype(bf16)
    cols[...] = (
        product(left_some[...].reshape(half_rows, size), mixed[...])
        .astype(bf16)
        .reshape(cols.shape)
    )

    def out_copy(to, sender):
        return remote(
            cols.at[to], update.at[:, columns(sender)], out_send.at[to], out_recv.at[sender],
            2 * to + half,
        )

    in_turn(lambda to: out_copy(to, chip).start(), 0)
    keep = pltpu.make_async_copy(cols.at[chip], update.at[:, columns(chip)], local_sem.at[5])
    keep.start()

    remote(
        left_stats, stat.at[rows_of(1 - half)], pair_send.at[2], pair_recv.at[2], partner
    ).wait_recv()
    pltpu.make_async_copy(left_stats, stat.at[rows_of(half)], local_sem.at[3]).wait()
    pltpu.make_async_copy(right_stats, other, local_sem.at[4]).wait()

    def blend(old, gram):
        return decay * old + (1.0 - decay) * gram

    @pl.when(half == 0)
    def _():
        g = block[...].reshape(size, size)
        stat[...] = blend(
            stat[...], lax.dot_general(g, g, ROWS_BY_ROWS, preferred_element_type=f32)
        )
        new_left[...] = stat[:half_rows]
        new_right[...] = blend(
            other[...],
            lax.dot_general(g[:, :half_rows], g, COLS_BY_COLS, preferred_element_type=f32),
        )

    @pl.when(half == 1)
    def _():
        g = block[...].reshape(size, size)
        stat[...] = blend(
            stat[...], lax.dot_general(g, g, COLS_BY_COLS, preferred_element_type=f32)
        )
        new_right[...] = stat[half_rows:]
        new_left[...] = blend(
            other[...],
            lax.dot_general(g[half_rows:], g, ROWS_BY_ROWS, preferred_element_type=f32),
        )

    root_into(root, stat, (moment, lead, tail, m16, n16, h16, p16, v16, q16))
    give = remote(root.at[rows_of(1 - half)], taken, pair_send.at[3], pair_recv.at[3], partner)
    give.start()

    @pl.when(half == 0)
    def _():
        fresh_left[...] = root[:half_rows]

    @pl.when(half == 1)
    def _():
        fresh_right[...] = root[half_rows:]

    give.wait_recv()

    @pl.when(half == 0)
    def _():
        fresh_right[...] = taken[...]

    @pl.when(half == 1)
    def _():
        fresh_left[...] = taken[...]

    keep.wait()
    for offset in near:
        out_copy(peer(offset), peer(offset)).wait_recv()
    for offset in near:
        in_copy(peer(offset), chip).wait_send()
        pass_on(peer(offset)).wait_send()
        out_copy(peer(offset), chip).wait_send()
    pair_own.wait_send()
    pair_right.wait_send()
    pair_left.wait_send()
    pair_stat(left_stats).wait_send()
    give.wait_send()


def final_kernel(
    refresh, update, new_left, new_right, fresh_left, fresh_right, old_left, old_right,
    update_out, left_out, right_out, left_root, right_root, chosen, sems,
):
    block_col = lax.div(lax.axis_index("bcol"), 2)
    fetched = pltpu.make_async_copy(refresh, chosen, sems.at[5])
    fetched.start()
    sure = [
        pltpu.make_async_copy(update, update_out, sems.at[0]),
        pltpu.make_async_copy(new_left, left_out, sems.at[1]),
        pltpu.make_async_copy(new_right, right_out, sems.at[2]),
    ]
    for copy in sure:
        copy.start()
    fetched.wait()
    listed = chosen[0, 0] == block_col
    for place in range(1, chosen.shape[1]):
        listed = jnp.logical_or(listed, chosen[0, place] == block_col)

    @pl.when(listed)
    def _():
        pltpu.make_async_copy(fresh_left, left_root, sems.at[3]).start()
        pltpu.make_async_copy(fresh_right, right_root, sems.at[4]).start()

    @pl.when(jnp.logical_not(listed))
    def _():
        pltpu.make_async_copy(old_left, left_root, sems.at[3]).start()
        pltpu.make_async_copy(old_right, right_root, sems.at[4]).start()

    for copy in sure:
        copy.wait()
    pltpu.make_async_copy(fresh_left, left_root, sems.at[3]).wait()
    pltpu.make_async_copy(fresh_right, right_root, sems.at[4]).wait()


def body(chips, gradient, left_stats, right_stats, left_roots, right_roots, refresh):
    slab_rows, half_rows, size = gradient.shape[0], left_stats.shape[1], left_stats.shape[2]
    width = gradient.shape[1]
    per_half = chips // 2
    place = functools.partial(pltpu.with_memory_space_constraint, memory_space=pltpu.HBM)
    in_hbm = pl.BlockSpec(memory_space=pltpu.HBM)
    in_vmem = pl.BlockSpec(memory_space=pltpu.VMEM)
    shaped = jax.ShapeDtypeStruct
    dma = pltpu.SemaphoreType.DMA
    square32, square16 = pltpu.VMEM((size, size), f32), pltpu.VMEM((size, size), bf16)
    stat_half = shaped((half_rows, size), f32)
    root_half = shaped((half_rows, size), bf16)
    results = pl.pallas_call(
        step_kernel,
        out_shape=(shaped((slab_rows, width), bf16), stat_half, stat_half, root_half, root_half),
        in_specs=[in_hbm] * 5,
        out_specs=[in_vmem] * 5,
        scratch_shapes=[
            pltpu.VMEM((2 * chips, slab_rows, size), bf16),
            pltpu.VMEM((chips, slab_rows, size), bf16),
            square16,
            square32,
            pltpu.VMEM((half_rows, size), f32),
            square16,
            pltpu.VMEM((chips, slab_rows, size), bf16),
            square16,
            pltpu.VMEM((half_rows, size), bf16),
            square32, square32, square32,
            square16, square16, square16, square16, square16, square16,
            dma((chips,)), dma((chips,)), dma((chips,)), dma((chips,)),
            dma((chips,)), dma((chips,)), dma((4,)), dma((4,)), dma((6,)),
        ],
        compiler_params=pltpu.CompilerParams(
            collective_id=0, has_side_effects=True, vmem_limit_bytes=40 * 2**20
        ),
        name="exchange",
    )(
        place(gradient),
        place(left_stats[0]),
        place(right_stats[0]),
        place(left_roots.reshape(per_half, 2, slab_rows, size)),
        place(right_roots[0]),
    )
    outputs = pl.pallas_call(
        final_kernel,
        out_shape=(shaped((slab_rows, width), bf16), stat_half, stat_half, root_half, root_half),
        in_specs=[in_hbm] + [pl.BlockSpec(memory_space=pl.ANY)] * 7,
        out_specs=[in_hbm] * 5,
        scratch_shapes=[pltpu.SMEM(refresh.shape, jnp.int32), dma((6,))],
        compiler_params=pltpu.CompilerParams(vmem_limit_bytes=2**20),
        name="place",
    )(place(refresh), *results, left_roots[0], right_roots[0])
    return (outputs[0],) + tuple(out[None] for out in outputs[1:])


def solution(mesh):
    rows, blocks = P(("brow", "bcol"), None), P("brow", "bcol", None)
    return jax.shard_map(
        functools.partial(body, mesh.shape["bcol"] // 2),
        mesh=mesh,
        in_specs=(rows, blocks, blocks, blocks, blocks, P("brow", None)),
        out_specs=(rows, blocks, blocks, blocks, blocks),
        check_vma=False,
    )
```

```python
import functools

import jax
import jax.numpy as jnp
from jax import lax
from jax.experimental import pallas as pl
from jax.experimental.pallas import tpu as pltpu
from jax.sharding import PartitionSpec as P

MESH = pl.DeviceIdType.MESH
bf16 = jnp.bfloat16
f32 = jnp.float32

decay = 0.9
epsilon = 1e-06
IN_FLIGHT = 4
OUT_FLIGHT = 8
LEAD = 1.25

ROWS_BY_ROWS = (((1,), (1,)), ((), ()))
COLS_BY_COLS = (((0,), (0,)), ((), ()))


def product(left_side, right_side):
    return jnp.dot(left_side, right_side, preferred_element_type=f32)


def begins(chips, chip):
    if 2 * chip < chips:
        return chip
    if 4 * chip >= 3 * chips:
        return 2 * chips - 1 - chip
    return chips / 2 + chip + 2.4


def root_into(root_ref, stat_ref, held, step):
    moment, lead, tail, m16, n16, h16, p16, v16, q16 = held
    size = stat_ref.shape[0]
    a = LEAD
    diagonal = lax.broadcasted_iota(jnp.int32, (size, size), 0) == lax.broadcasted_iota(
        jnp.int32, (size, size), 1
    )
    shifted = stat_ref[...] + jnp.where(diagonal, epsilon, 0.0)
    total = jnp.sum(jnp.sum(shifted * shifted, axis=0, keepdims=True), axis=1, keepdims=True)
    scaling = 2.5 / jnp.sqrt(total)
    scale = jnp.sqrt(jnp.sqrt(scaling))
    moment[...] = shifted * scaling
    m16[...] = moment[...].astype(bf16)
    tail[...] = product(m16[...], m16[...])
    step()
    lead[...] = a * moment[...] - 0.25 * tail[...]
    h16[...] = lead[...].astype(bf16)
    tail[...] = 0.0625 * tail[...] - (0.5 * a) * moment[...]
    n16[...] = tail[...].astype(bf16)
    p16[...] = (2.0 * a * a * tail[...] + product(n16[...], n16[...])).astype(bf16)
    step()
    tail[...] = -0.25 * (a * moment[...] + a**4 * lead[...] + product(p16[...], h16[...]))
    v16[...] = tail[...].astype(bf16)
    step()
    q16[...] = (2.0 * a * a * tail[...] + product(v16[...], v16[...])).astype(bf16)
    step()
    lead[...] = a * a * moment[...] + product(v16[...], m16[...])
    h16[...] = lead[...].astype(bf16)
    step()
    lead[...] = a**4 * lead[...] + product(q16[...], h16[...])
    h16[...] = lead[...].astype(bf16)
    lead[...] = a**4 * lead[...] + product(q16[...], h16[...])
    root = jnp.where(diagonal, a**3, 0.0) + a * tail[...] - 0.25 * lead[...]
    root_ref[...] = (scale * root).astype(bf16)


def step_kernel(
    grad, left_stats, right_stats, left_roots, right_roots,
    update, new_left, new_right, fresh_left, fresh_right,
    block, left_some, right_whole, stat, other, mixed, cols, root, taken,
    moment, lead, tail, m16, n16, h16, p16, v16, q16,
    in_send, in_recv, pass_send, pass_recv, out_send, out_recv,
    pair_send, pair_recv, local_sem,
):
    slabs, slab_rows, size = block.shape
    chips, half_rows = slabs // 2, size // 2
    per_half = chips // 2
    me = lax.axis_index("bcol")
    chip, half = lax.div(me, 2), lax.rem(me, 2)
    partner = 2 * chip + (1 - half)
    near = [d * s for d in range(1, chips // 2) for s in (1, -1)] + [chips // 2]

    def peer(offset):
        return lax.rem(chip + (offset + chips), chips)

    def remote(src, dst, send, recv, target):
        return pltpu.make_async_remote_copy(
            src_ref=src, dst_ref=dst, send_sem=send, recv_sem=recv,
            device_id={"bcol": target}, device_id_type=MESH,
        )

    def even_first(parity):
        return [o for turn in (0, 1) for o in near[::-1] if (parity + o) % 2 == turn]

    def gather_rows(copy):
        for parity in (0, 1):

            @pl.when(lax.rem(chip, 2) == parity)
            def _():
                order = even_first(parity)
                for place, offset in enumerate(order):
                    if place >= IN_FLIGHT:
                        copy(peer(order[place - IN_FLIGHT])).wait_send()
                    copy(peer(offset)).start()

    def gather_rest(copy):
        for parity in (0, 1):

            @pl.when(lax.rem(chip, 2) == parity)
            def _():
                for offset in even_first(parity)[-IN_FLIGHT:]:
                    copy(peer(offset)).wait_send()

    def columns(index):
        return pl.ds(pl.multiple_of(index * size, size), size)

    def rows_of(index):
        return pl.ds(pl.multiple_of(index * half_rows, half_rows), half_rows)

    barrier = pltpu.get_barrier_semaphore()
    for offset in near:
        pl.semaphore_signal(
            barrier, inc=1, device_id={"bcol": 2 * peer(offset) + half}, device_id_type=MESH
        )
    pl.semaphore_signal(barrier, inc=1, device_id={"bcol": partner}, device_id_type=MESH)

    own_block = pltpu.make_async_copy(grad.at[:, columns(chip)], block.at[me], local_sem.at[0])
    own_left = pltpu.make_async_copy(
        left_roots.at[:, half], left_some.at[pl.ds(half * per_half, per_half)], local_sem.at[1]
    )
    own_right = pltpu.make_async_copy(right_roots, right_whole.at[rows_of(half)], local_sem.at[2])
    own_block.start()
    own_left.start()
    own_right.start()

    @pl.when(half == 0)
    def _():
        pltpu.make_async_copy(left_stats, stat.at[rows_of(half)], local_sem.at[3]).start()
        pltpu.make_async_copy(right_stats, other, local_sem.at[4]).start()

    @pl.when(half == 1)
    def _():
        pltpu.make_async_copy(right_stats, stat.at[rows_of(half)], local_sem.at[3]).start()
        pltpu.make_async_copy(left_stats, other, local_sem.at[4]).start()

    pl.semaphore_wait(barrier, chips)

    pair_own = remote(
        grad.at[:, columns(chip)], block.at[me], pass_send.at[chip], pass_recv.at[chip], partner
    )
    pair_right = remote(
        right_roots, right_whole.at[rows_of(half)], pair_send.at[0], pair_recv.at[0], partner
    )
    pair_left = remote(
        left_roots.at[:, 1 - half], left_some.at[pl.ds(half * per_half, per_half)],
        pair_send.at[1], pair_recv.at[1], partner,
    )

    def pair_stat(source):
        return remote(source, stat.at[rows_of(half)], pair_send.at[2], pair_recv.at[2], partner)

    pair_own.start()
    pair_right.start()
    pair_left.start()

    def in_copy(to, sender):
        return remote(
            grad.at[:, columns(to)], block.at[2 * sender + half],
            in_send.at[to], in_recv.at[sender], 2 * to + half,
        )

    gather_rows(lambda to: in_copy(to, chip))

    @pl.when(half == 0)
    def _():
        pair_stat(right_stats).start()

    @pl.when(half == 1)
    def _():
        pair_stat(left_stats).start()

    def pass_on(sender):
        slot = block.at[2 * sender + half]
        return remote(slot, slot, pass_send.at[sender], pass_recv.at[sender], partner)

    def passed(sender):
        slot = block.at[2 * sender + (1 - half)]
        return remote(slot, slot, pass_send.at[sender], pass_recv.at[sender], partner)

    for offset in near[::-1]:
        sender = peer(offset)
        in_copy(sender, sender).wait_recv()
        pass_on(sender).start()

    own_right.wait()
    own_left.wait()
    own_block.wait()
    remote(
        right_roots, right_whole.at[rows_of(1 - half)], pair_send.at[0], pair_recv.at[0], partner
    ).wait_recv()
    remote(
        left_roots.at[:, 1 - half], left_some.at[pl.ds((1 - half) * per_half, per_half)],
        pair_send.at[1], pair_recv.at[1], partner,
    ).wait_recv()
    passed(chip).wait_recv()
    for offset in near:
        passed(peer(offset)).wait_recv()

    whole = block[...].reshape(size, size)
    mixed[...] = product(whole, right_whole[...]).astype(bf16)
    cols[...] = (
        product(left_some[...].reshape(half_rows, size), mixed[...])
        .astype(bf16)
        .reshape(cols.shape)
    )

    def out_copy(to, sender):
        return remote(
            cols.at[to], update.at[:, columns(sender)], out_send.at[to], out_recv.at[sender],
            2 * to + half,
        )

    def out_step(place):
        if place >= OUT_FLIGHT:
            out_left(place - OUT_FLIGHT)
        if place < chips:

            @pl.when(chip != turns[place])
            def _():
                out_copy(turns[place], chip).start()

    def out_left(place):
        @pl.when(chip != turns[place])
        def _():
            out_copy(turns[place], chip).wait_send()

    turns = sorted(range(chips), key=functools.partial(begins, chips))
    for place in range(OUT_FLIGHT):
        out_step(place)
    places = iter(range(OUT_FLIGHT, chips + OUT_FLIGHT))

    def step():
        place = next(places, None)
        if place is not None:
            out_step(place)

    keep = pltpu.make_async_copy(cols.at[chip], update.at[:, columns(chip)], local_sem.at[5])
    keep.start()

    remote(
        left_stats, stat.at[rows_of(1 - half)], pair_send.at[2], pair_recv.at[2], partner
    ).wait_recv()
    pltpu.make_async_copy(left_stats, stat.at[rows_of(half)], local_sem.at[3]).wait()
    pltpu.make_async_copy(right_stats, other, local_sem.at[4]).wait()

    def blend(old, gram):
        return decay * old + (1.0 - decay) * gram

    @pl.when(half == 0)
    def _():
        g = block[...].reshape(size, size)
        stat[...] = blend(
            stat[...], lax.dot_general(g, g, ROWS_BY_ROWS, preferred_element_type=f32)
        )
        new_left[...] = stat[:half_rows]
        new_right[...] = blend(
            other[...],
            lax.dot_general(g[:, :half_rows], g, COLS_BY_COLS, preferred_element_type=f32),
        )

    @pl.when(half == 1)
    def _():
        g = block[...].reshape(size, size)
        stat[...] = blend(
            stat[...], lax.dot_general(g, g, COLS_BY_COLS, preferred_element_type=f32)
        )
        new_right[...] = stat[half_rows:]
        new_left[...] = blend(
            other[...],
            lax.dot_general(g[half_rows:], g, ROWS_BY_ROWS, preferred_element_type=f32),
        )

    step()
    root_into(root, stat, (moment, lead, tail, m16, n16, h16, p16, v16, q16), step)
    give = remote(root.at[rows_of(1 - half)], taken, pair_send.at[3], pair_recv.at[3], partner)
    give.start()
    step()
    step()

    @pl.when(half == 0)
    def _():
        fresh_left[...] = root[:half_rows]

    @pl.when(half == 1)
    def _():
        fresh_right[...] = root[half_rows:]

    for place in places:
        out_step(place)
    give.wait_recv()

    @pl.when(half == 0)
    def _():
        fresh_right[...] = taken[...]

    @pl.when(half == 1)
    def _():
        fresh_left[...] = taken[...]

    keep.wait()
    for offset in near:
        out_copy(peer(offset), peer(offset)).wait_recv()
    for offset in near:
        pass_on(peer(offset)).wait_send()
    gather_rest(lambda to: in_copy(to, chip))
    pair_own.wait_send()
    pair_right.wait_send()
    pair_left.wait_send()
    pair_stat(left_stats).wait_send()
    give.wait_send()


def final_kernel(
    refresh, update, new_left, new_right, fresh_left, fresh_right, old_left, old_right,
    update_out, left_out, right_out, left_root, right_root, chosen, sems,
):
    block_col = lax.div(lax.axis_index("bcol"), 2)
    fetched = pltpu.make_async_copy(refresh, chosen, sems.at[5])
    fetched.start()
    sure = [
        pltpu.make_async_copy(update, update_out, sems.at[0]),
        pltpu.make_async_copy(new_left, left_out, sems.at[1]),
        pltpu.make_async_copy(new_right, right_out, sems.at[2]),
    ]
    for copy in sure:
        copy.start()
    fetched.wait()
    listed = chosen[0, 0] == block_col
    for place in range(1, chosen.shape[1]):
        listed = jnp.logical_or(listed, chosen[0, place] == block_col)

    @pl.when(listed)
    def _():
        pltpu.make_async_copy(fresh_left, left_root, sems.at[3]).start()
        pltpu.make_async_copy(fresh_right, right_root, sems.at[4]).start()

    @pl.when(jnp.logical_not(listed))
    def _():
        pltpu.make_async_copy(old_left, left_root, sems.at[3]).start()
        pltpu.make_async_copy(old_right, right_root, sems.at[4]).start()

    for copy in sure:
        copy.wait()
    pltpu.make_async_copy(fresh_left, left_root, sems.at[3]).wait()
    pltpu.make_async_copy(fresh_right, right_root, sems.at[4]).wait()


def body(chips, gradient, left_stats, right_stats, left_roots, right_roots, refresh):
    slab_rows, half_rows, size = gradient.shape[0], left_stats.shape[1], left_stats.shape[2]
    width = gradient.shape[1]
    per_half = chips // 2
    place = functools.partial(pltpu.with_memory_space_constraint, memory_space=pltpu.HBM)
    in_hbm = pl.BlockSpec(memory_space=pltpu.HBM)
    in_vmem = pl.BlockSpec(memory_space=pltpu.VMEM)
    shaped = jax.ShapeDtypeStruct
    dma = pltpu.SemaphoreType.DMA
    square32, square16 = pltpu.VMEM((size, size), f32), pltpu.VMEM((size, size), bf16)
    stat_half = shaped((half_rows, size), f32)
    root_half = shaped((half_rows, size), bf16)
    results = pl.pallas_call(
        step_kernel,
        out_shape=(shaped((slab_rows, width), bf16), stat_half, stat_half, root_half, root_half),
        in_specs=[in_hbm] * 5,
        out_specs=[in_vmem] * 5,
        scratch_shapes=[
            pltpu.VMEM((2 * chips, slab_rows, size), bf16),
            pltpu.VMEM((chips, slab_rows, size), bf16),
            square16,
            square32,
            pltpu.VMEM((half_rows, size), f32),
            square16,
            pltpu.VMEM((chips, slab_rows, size), bf16),
            square16,
            pltpu.VMEM((half_rows, size), bf16),
            square32, square32, square32,
            square16, square16, square16, square16, square16, square16,
            dma((chips,)), dma((chips,)), dma((chips,)), dma((chips,)),
            dma((chips,)), dma((chips,)), dma((4,)), dma((4,)), dma((6,)),
        ],
        compiler_params=pltpu.CompilerParams(
            collective_id=0, has_side_effects=True, vmem_limit_bytes=40 * 2**20
        ),
        name="exchange",
    )(
        place(gradient),
        place(left_stats[0]),
        place(right_stats[0]),
        place(left_roots.reshape(per_half, 2, slab_rows, size)),
        place(right_roots[0]),
    )
    outputs = pl.pallas_call(
        final_kernel,
        out_shape=(shaped((slab_rows, width), bf16), stat_half, stat_half, root_half, root_half),
        in_specs=[in_hbm] + [pl.BlockSpec(memory_space=pl.ANY)] * 7,
        out_specs=[in_hbm] * 5,
        scratch_shapes=[pltpu.SMEM(refresh.shape, jnp.int32), dma((6,))],
        compiler_params=pltpu.CompilerParams(vmem_limit_bytes=2**20),
        name="place",
    )(place(refresh), *results, left_roots[0], right_roots[0])
    return (outputs[0],) + tuple(out[None] for out in outputs[1:])


def solution(mesh):
    rows, blocks = P(("brow", "bcol"), None), P("brow", "bcol", None)
    return jax.shard_map(
        functools.partial(body, mesh.shape["bcol"] // 2),
        mesh=mesh,
        in_specs=(rows, blocks, blocks, blocks, blocks, P("brow", None)),
        out_specs=(rows, blocks, blocks, blocks, blocks),
        check_vma=False,
    )
```

```python
import functools

import jax
import jax.numpy as jnp
from jax import lax
from jax.experimental import pallas as pl
from jax.experimental.pallas import tpu as pltpu
from jax.sharding import PartitionSpec as P

MESH = pl.DeviceIdType.MESH
bf16 = jnp.bfloat16
f32 = jnp.float32

decay = 0.9
epsilon = 1e-06
IN_FLIGHT = 4
OUT_FLIGHT = 8
LEAD = 1.25

ROWS_BY_ROWS = (((1,), (1,)), ((), ()))
COLS_BY_COLS = (((0,), (0,)), ((), ()))


def product(left_side, right_side):
    return jnp.dot(left_side, right_side, preferred_element_type=f32)


def begins(chips, chip):
    if 2 * chip < chips:
        return chip
    if 4 * chip >= 3 * chips:
        return 2 * chips - chip - 0.5
    return chips / 2 + chip


def root_into(root_ref, stat_ref, held, step):
    moment, lead, tail, m16, n16, h16, p16, v16, q16 = held
    size = stat_ref.shape[0]
    a = LEAD
    diagonal = lax.broadcasted_iota(jnp.int32, (size, size), 0) == lax.broadcasted_iota(
        jnp.int32, (size, size), 1
    )
    shifted = stat_ref[...] + jnp.where(diagonal, epsilon, 0.0)
    total = jnp.sum(jnp.sum(shifted * shifted, axis=0, keepdims=True), axis=1, keepdims=True)
    scaling = 2.5 / jnp.sqrt(total)
    scale = jnp.sqrt(jnp.sqrt(scaling))
    moment[...] = shifted * scaling
    m16[...] = moment[...].astype(bf16)
    tail[...] = product(m16[...], m16[...])
    step()
    lead[...] = a * moment[...] - 0.25 * tail[...]
    h16[...] = lead[...].astype(bf16)
    tail[...] = 0.0625 * tail[...] - (0.5 * a) * moment[...]
    n16[...] = tail[...].astype(bf16)
    p16[...] = (2.0 * a * a * tail[...] + product(n16[...], n16[...])).astype(bf16)
    step()
    tail[...] = -0.25 * (a * moment[...] + a**4 * lead[...] + product(p16[...], h16[...]))
    v16[...] = tail[...].astype(bf16)
    step()
    q16[...] = (2.0 * a * a * tail[...] + product(v16[...], v16[...])).astype(bf16)
    step()
    lead[...] = a * a * moment[...] + product(v16[...], m16[...])
    h16[...] = lead[...].astype(bf16)
    step()
    lead[...] = a**4 * lead[...] + product(q16[...], h16[...])
    h16[...] = lead[...].astype(bf16)
    lead[...] = a**4 * lead[...] + product(q16[...], h16[...])
    root = jnp.where(diagonal, a**3, 0.0) + a * tail[...] - 0.25 * lead[...]
    root_ref[...] = (scale * root).astype(bf16)


def step_kernel(
    grad, left_stats, right_stats, left_roots, right_roots,
    update, new_left, new_right, fresh_left, fresh_right,
    block, left_some, right_whole, stat, other, mixed, cols, root, taken,
    moment, lead, tail, m16, n16, h16, p16, v16, q16,
    in_send, in_recv, pass_send, pass_recv, out_send, out_recv,
    pair_send, pair_recv, local_sem,
):
    slabs, slab_rows, size = block.shape
    chips, half_rows = slabs // 2, size // 2
    per_half = chips // 2
    me = lax.axis_index("bcol")
    chip, half = lax.div(me, 2), lax.rem(me, 2)
    partner = 2 * chip + (1 - half)
    near = [d * s for d in range(1, chips // 2) for s in (1, -1)] + [chips // 2]

    def peer(offset):
        return lax.rem(chip + (offset + chips), chips)

    def remote(src, dst, send, recv, target):
        return pltpu.make_async_remote_copy(
            src_ref=src, dst_ref=dst, send_sem=send, recv_sem=recv,
            device_id={"bcol": target}, device_id_type=MESH,
        )

    def even_first(parity):
        return [o for turn in (0, 1) for o in near[::-1] if (parity + o) % 2 == turn]

    def gather_rows(copy):
        for parity in (0, 1):

            @pl.when(lax.rem(chip, 2) == parity)
            def _():
                order = even_first(parity)
                for place, offset in enumerate(order):
                    if place >= IN_FLIGHT:
                        copy(peer(order[place - IN_FLIGHT])).wait_send()
                    copy(peer(offset)).start()
                    if place == min(IN_FLIGHT, len(order)) - 1:
                        share()

    def gather_rest(copy):
        for parity in (0, 1):

            @pl.when(lax.rem(chip, 2) == parity)
            def _():
                for offset in even_first(parity)[-IN_FLIGHT:]:
                    copy(peer(offset)).wait_send()

    def columns(index):
        return pl.ds(pl.multiple_of(index * size, size), size)

    def rows_of(index):
        return pl.ds(pl.multiple_of(index * half_rows, half_rows), half_rows)

    barrier = pltpu.get_barrier_semaphore()
    for offset in near:
        pl.semaphore_signal(
            barrier, inc=1, device_id={"bcol": 2 * peer(offset) + half}, device_id_type=MESH
        )
    pl.semaphore_signal(barrier, inc=1, device_id={"bcol": partner}, device_id_type=MESH)

    own_block = pltpu.make_async_copy(grad.at[:, columns(chip)], block.at[me], local_sem.at[0])
    own_left = pltpu.make_async_copy(
        left_roots.at[:, half], left_some.at[pl.ds(half * per_half, per_half)], local_sem.at[1]
    )
    own_right = pltpu.make_async_copy(right_roots, right_whole.at[rows_of(half)], local_sem.at[2])

    pl.semaphore_wait(barrier, chips)

    pair_own = remote(
        grad.at[:, columns(chip)], block.at[me], pass_send.at[chip], pass_recv.at[chip], partner
    )
    pair_right = remote(
        right_roots, right_whole.at[rows_of(half)], pair_send.at[0], pair_recv.at[0], partner
    )
    pair_left = remote(
        left_roots.at[:, 1 - half], left_some.at[pl.ds(half * per_half, per_half)],
        pair_send.at[1], pair_recv.at[1], partner,
    )

    def pair_stat(source):
        return remote(source, stat.at[rows_of(half)], pair_send.at[2], pair_recv.at[2], partner)

    def share():
        own_block.start()
        own_left.start()
        own_right.start()

        @pl.when(half == 0)
        def _():
            pltpu.make_async_copy(left_stats, stat.at[rows_of(half)], local_sem.at[3]).start()
            pltpu.make_async_copy(right_stats, other, local_sem.at[4]).start()

        @pl.when(half == 1)
        def _():
            pltpu.make_async_copy(right_stats, stat.at[rows_of(half)], local_sem.at[3]).start()
            pltpu.make_async_copy(left_stats, other, local_sem.at[4]).start()
        pair_own.start()
        pair_right.start()
        pair_left.start()

        @pl.when(half == 0)
        def _():
            pair_stat(right_stats).start()

        @pl.when(half == 1)
        def _():
            pair_stat(left_stats).start()

    def in_copy(to, sender):
        return remote(
            grad.at[:, columns(to)], block.at[2 * sender + half],
            in_send.at[to], in_recv.at[sender], 2 * to + half,
        )

    gather_rows(lambda to: in_copy(to, chip))

    def pass_on(sender):
        slot = block.at[2 * sender + half]
        return remote(slot, slot, pass_send.at[sender], pass_recv.at[sender], partner)

    def passed(sender):
        slot = block.at[2 * sender + (1 - half)]
        return remote(slot, slot, pass_send.at[sender], pass_recv.at[sender], partner)

    for offset in near[::-1]:
        sender = peer(offset)
        in_copy(sender, sender).wait_recv()
        pass_on(sender).start()

    own_right.wait()
    own_left.wait()
    own_block.wait()
    remote(
        right_roots, right_whole.at[rows_of(1 - half)], pair_send.at[0], pair_recv.at[0], partner
    ).wait_recv()
    remote(
        left_roots.at[:, 1 - half], left_some.at[pl.ds((1 - half) * per_half, per_half)],
        pair_send.at[1], pair_recv.at[1], partner,
    ).wait_recv()
    passed(chip).wait_recv()
    for offset in near:
        passed(peer(offset)).wait_recv()

    whole = block[...].reshape(size, size)
    mixed[...] = product(whole, right_whole[...]).astype(bf16)

    def update_rows(first, count):
        part = left_some[pl.ds(first, count)].reshape(count * slab_rows, size)
        part = product(part, mixed[...]).astype(bf16)
        cols[pl.ds(first, count)] = part.reshape(count, slab_rows, size)

    def out_copy(to, sender):
        return remote(
            cols.at[to], update.at[:, columns(sender)], out_send.at[to], out_recv.at[sender],
            2 * to + half,
        )

    def out_step(place):
        if place >= OUT_FLIGHT:
            out_left(place - OUT_FLIGHT)
        if place < chips:

            @pl.when(chip != turns[place])
            def _():
                out_copy(turns[place], chip).start()

    def out_left(place):
        @pl.when(chip != turns[place])
        def _():
            out_copy(turns[place], chip).wait_send()

    turns = sorted(range(chips), key=functools.partial(begins, chips))
    update_rows(0, per_half)
    for place in range(min(OUT_FLIGHT, per_half)):
        out_step(place)
    update_rows(per_half, per_half)
    for place in range(min(OUT_FLIGHT, per_half), OUT_FLIGHT):
        out_step(place)
    places = iter(range(OUT_FLIGHT, chips + OUT_FLIGHT))

    def step():
        place = next(places, None)
        if place is not None:
            out_step(place)

    keep = pltpu.make_async_copy(cols.at[chip], update.at[:, columns(chip)], local_sem.at[5])
    keep.start()

    remote(
        left_stats, stat.at[rows_of(1 - half)], pair_send.at[2], pair_recv.at[2], partner
    ).wait_recv()
    pltpu.make_async_copy(left_stats, stat.at[rows_of(half)], local_sem.at[3]).wait()
    pltpu.make_async_copy(right_stats, other, local_sem.at[4]).wait()

    def blend(old, gram):
        return decay * old + (1.0 - decay) * gram

    @pl.when(half == 0)
    def _():
        g = block[...].reshape(size, size)
        stat[...] = blend(
            stat[...], lax.dot_general(g, g, ROWS_BY_ROWS, preferred_element_type=f32)
        )
        new_left[...] = stat[:half_rows]
        new_right[...] = blend(
            other[...],
            lax.dot_general(g[:, :half_rows], g, COLS_BY_COLS, preferred_element_type=f32),
        )

    @pl.when(half == 1)
    def _():
        g = block[...].reshape(size, size)
        stat[...] = blend(
            stat[...], lax.dot_general(g, g, COLS_BY_COLS, preferred_element_type=f32)
        )
        new_right[...] = stat[half_rows:]
        new_left[...] = blend(
            other[...],
            lax.dot_general(g[half_rows:], g, ROWS_BY_ROWS, preferred_element_type=f32),
        )

    step()
    root_into(root, stat, (moment, lead, tail, m16, n16, h16, p16, v16, q16), step)
    give = remote(root.at[rows_of(1 - half)], taken, pair_send.at[3], pair_recv.at[3], partner)
    give.start()
    step()
    step()

    @pl.when(half == 0)
    def _():
        fresh_left[...] = root[:half_rows]

    @pl.when(half == 1)
    def _():
        fresh_right[...] = root[half_rows:]

    for place in places:
        out_step(place)
    give.wait_recv()

    @pl.when(half == 0)
    def _():
        fresh_right[...] = taken[...]

    @pl.when(half == 1)
    def _():
        fresh_left[...] = taken[...]

    for offset in near:
        pass_on(peer(offset)).wait_send()
    gather_rest(lambda to: in_copy(to, chip))
    pair_own.wait_send()
    pair_right.wait_send()
    pair_left.wait_send()
    pair_stat(left_stats).wait_send()
    give.wait_send()
    keep.wait()
    for offset in near:
        out_copy(peer(offset), peer(offset)).wait_recv()


def final_kernel(
    refresh, update, new_left, new_right, fresh_left, fresh_right, old_left, old_right,
    update_out, left_out, right_out, left_root, right_root, chosen, sems,
):
    block_col = lax.div(lax.axis_index("bcol"), 2)
    fetched = pltpu.make_async_copy(refresh, chosen, sems.at[5])
    fetched.start()
    sure = [
        pltpu.make_async_copy(update, update_out, sems.at[0]),
        pltpu.make_async_copy(new_left, left_out, sems.at[1]),
        pltpu.make_async_copy(new_right, right_out, sems.at[2]),
    ]
    for copy in sure:
        copy.start()
    fetched.wait()
    listed = chosen[0, 0] == block_col
    for place in range(1, chosen.shape[1]):
        listed = jnp.logical_or(listed, chosen[0, place] == block_col)

    @pl.when(listed)
    def _():
        pltpu.make_async_copy(fresh_left, left_root, sems.at[3]).start()
        pltpu.make_async_copy(fresh_right, right_root, sems.at[4]).start()

    @pl.when(jnp.logical_not(listed))
    def _():
        pltpu.make_async_copy(old_left, left_root, sems.at[3]).start()
        pltpu.make_async_copy(old_right, right_root, sems.at[4]).start()

    for copy in sure:
        copy.wait()
    pltpu.make_async_copy(fresh_left, left_root, sems.at[3]).wait()
    pltpu.make_async_copy(fresh_right, right_root, sems.at[4]).wait()


def body(chips, gradient, left_stats, right_stats, left_roots, right_roots, refresh):
    slab_rows, half_rows, size = gradient.shape[0], left_stats.shape[1], left_stats.shape[2]
    width = gradient.shape[1]
    per_half = chips // 2
    place = functools.partial(pltpu.with_memory_space_constraint, memory_space=pltpu.HBM)
    in_hbm = pl.BlockSpec(memory_space=pltpu.HBM)
    in_vmem = pl.BlockSpec(memory_space=pltpu.VMEM)
    shaped = jax.ShapeDtypeStruct
    dma = pltpu.SemaphoreType.DMA
    square32, square16 = pltpu.VMEM((size, size), f32), pltpu.VMEM((size, size), bf16)
    stat_half = shaped((half_rows, size), f32)
    root_half = shaped((half_rows, size), bf16)
    results = pl.pallas_call(
        step_kernel,
        out_shape=(shaped((slab_rows, width), bf16), stat_half, stat_half, root_half, root_half),
        in_specs=[in_hbm] * 5,
        out_specs=[in_vmem] * 5,
        scratch_shapes=[
            pltpu.VMEM((2 * chips, slab_rows, size), bf16),
            pltpu.VMEM((chips, slab_rows, size), bf16),
            square16,
            square32,
            pltpu.VMEM((half_rows, size), f32),
            square16,
            pltpu.VMEM((chips, slab_rows, size), bf16),
            square16,
            pltpu.VMEM((half_rows, size), bf16),
            square32, square32, square32,
            square16, square16, square16, square16, square16, square16,
            dma((chips,)), dma((chips,)), dma((chips,)), dma((chips,)),
            dma((chips,)), dma((chips,)), dma((4,)), dma((4,)), dma((6,)),
        ],
        compiler_params=pltpu.CompilerParams(
            collective_id=0, has_side_effects=True, vmem_limit_bytes=40 * 2**20
        ),
        name="exchange",
    )(
        place(gradient),
        place(left_stats[0]),
        place(right_stats[0]),
        place(left_roots.reshape(per_half, 2, slab_rows, size)),
        place(right_roots[0]),
    )
    outputs = pl.pallas_call(
        final_kernel,
        out_shape=(shaped((slab_rows, width), bf16), stat_half, stat_half, root_half, root_half),
        in_specs=[in_hbm] + [pl.BlockSpec(memory_space=pl.ANY)] * 7,
        out_specs=[in_hbm] * 5,
        scratch_shapes=[pltpu.SMEM(refresh.shape, jnp.int32), dma((6,))],
        compiler_params=pltpu.CompilerParams(vmem_limit_bytes=2**20),
        name="place",
    )(place(refresh), *results, left_roots[0], right_roots[0])
    return (outputs[0],) + tuple(out[None] for out in outputs[1:])


def solution(mesh):
    rows, blocks = P(("brow", "bcol"), None), P("brow", "bcol", None)
    return jax.shard_map(
        functools.partial(body, mesh.shape["bcol"] // 2),
        mesh=mesh,
        in_specs=(rows, blocks, blocks, blocks, blocks, P("brow", None)),
        out_specs=(rows, blocks, blocks, blocks, blocks),
        check_vma=False,
    )
```
